32 devices in a mesh: pipe: 2 (over core), dp: 4 (over y, x), expert: 4 (over z).
Axes of the slice: x: 2, y: 2, z: 4, core: 2. Of those that a mesh axis runs over, the one named last changes fastest.
Arguments:
- inputs: bfloat16 [2, 16, 64, 1024], P(None, ('dp', 'expert')), may hold values from -6 to 6
- cotangent: bfloat16 [2, 16, 64, 1024], P(None, ('dp', 'expert')), may hold values from -6 to 6
- segments: int32 [2, 16, 64], P(None, ('dp', 'expert')), may hold values from 0 to 3, never falling along the last dimension, each value on 1 to 32 neighbouring positions
- routes: int32 [2, 2, 16, 64, 8], P('pipe', None, ('dp', 'expert')), may hold values from 0 to 31, all different within a row; in each aligned block of 64 rows (0 to 63, 64 to 127, ..., all dimensions but the last counted through in order) at most 20 rows name the same one
- norm_attn: float32 [2, 1024], P('pipe'), may hold values from 0.5 to 1.5
- w_query: bfloat16 [2, 1024, 1024], P('pipe', 'dp'), may hold values from -0.1875 to 0.1875
- key_value_weight: bfloat16 [2, 1024, 1024], P('pipe', 'dp'), may hold values from -0.1875 to 0.1875
- w_out: bfloat16 [2, 1024, 1024], P('pipe', 'dp'), may hold values from -0.75 to 0.75
- norm_ffn: float32 [2, 1024], P('pipe'), may hold values from 0.5 to 1.5
- w_router: bfloat16 [2, 1024, 32], P('pipe'), may hold values from -0.09375 to 0.09375
- w_gate: bfloat16 [2, 32, 1024, 512], P('pipe', 'expert'), may hold values from -0.1875 to 0.1875
- w_up: bfloat16 [2, 32, 1024, 512], P('pipe', 'expert'), may hold values from -0.1875 to 0.1875
- w_down: bfloat16 [2, 32, 512, 1024], P('pipe', 'expert'), may hold values from -1 to 1
Outputs:
- hidden: float32 [2, 2, 16, 64, 1024], P('pipe', None, ('dp', 'expert'))
- grad_input: float32 [2, 2, 16, 64, 1024], P('pipe', None, ('dp', 'expert'))
- g_norm_attn: float32 [2, 1024], P('pipe', 'dp')
- g_query: float32 [2, 1024, 1024], P('pipe', 'dp')
- g_keyval: float32 [2, 1024, 1024], P('pipe', 'dp')
- g_out: float32 [2, 1024, 1024], P('pipe', 'dp')
- g_norm_ffn: float32 [2, 1024], P('pipe', 'dp')
- g_router: float32 [2, 1024, 32], P('pipe', 'dp')
- g_gate: float32 [2, 32, 1024, 512], P('pipe', 'expert', None, 'dp')
- g_up: float32 [2, 32, 1024, 512], P('pipe', 'expert', None, 'dp')
- g_down: float32 [2, 32, 512, 1024], P('pipe', 'expert', 'dp')
The draws below stay inside these ranges and needn't reach their ends.
Inputs may be any that keep to these rules, and one draw needn't show every extreme that they name: `routes`: within every block of 64 rows (the tokens of one sequence of one layer) no expert is named by more than 20 rows, a bound that some block reaches; a row names 8 different experts. `segments`: along every sequence segment numbers never fall; each segment holds 1 to 32 positions and one holds exactly 32.
All inputs are finite; a program needn't handle non-finite values.
Results may differ from the reference program's by a relative error of at most 0.028.
Values may be sent and summed in bfloat16 or wider, within the bound.
A program may use at most 256 MiB of HBM per device.

```python
import math
import jax
import jax.numpy as jnp
import numpy as np
from jax import lax

MODEL_DIMENSION = 1024
QUERY_HEADS = 16
KEY_VALUE_HEADS = 8
HEAD_DIMENSION = 64
EXPERTS = 32
FF = 512
TOP = 8
SEQ = 64
MICRO = 2
SEGS = 4
LAYER_COUNT = 2
BATCH = 16
CAP = 20


def block_levels(key, shape, cuts, smallest, high):
    level, own = 1.0, jax.random.fold_in(key, 6)
    for dim, parts in cuts:
        steps = jnp.exp(jax.random.uniform(jax.random.fold_in(own, dim), (parts,), jnp.float32, smallest / len(cuts), high / len(cuts)))
        level = level * jnp.repeat(steps, shape[dim] // parts).reshape([-1 if axis == dim else 1 for axis in range(len(shape))])
    return level


def profile(count, total, reach, lean):
    weights = [(1 << 20) // math.isqrt(grade ** lean) + 1 for grade in range(2, count + 1)]
    rest, counts = total - reach - (count - 1), [1] * (count - 1)
    while rest > 0:
        movable = [i for i in range(count - 1) if counts[i] < reach]
        whole, remaining = sum([weights[i] for i in movable]), rest
        for i in movable:
            addition = min(reach - counts[i], max(1, remaining * weights[i] // whole), rest)
            counts[i] = counts[i] + addition
            rest = rest - addition
    return np.array([reach] + counts)


def ragged(key, number_of, total, reach, slope):
    if number_of == 2:
        one = jax.random.randint(key, (), max(1, total - reach), min(reach, total - 1) + 1)
        return jnp.stack([one, total - one])
    sizes = jnp.asarray(profile(number_of, total, reach, slope), jnp.int32)
    twos = (number_of - 1) // 2
    donor, taker = sizes[1:1 + 2 * twos:2], sizes[2:2 + 2 * twos:2]
    slack = jnp.minimum(donor - 1, reach - taker)
    shifted = jax.random.randint(jax.random.fold_in(key, 1), (twos,), 0, 1 << 20) % (slack + 1)
    sizes = sizes.at[1:1 + 2 * twos:2].set(donor - shifted).at[2:2 + 2 * twos:2].set(taker + shifted)
    return sizes[jax.random.permutation(jax.random.fold_in(key, 2), number_of)]


def deal_out(key, own, number, rows, count, top, reach, skew):
    sequence = jax.random.permutation(key, count)
    crowded, usual = shares(count, rows * top, reach, skew, True), shares(count, rows * top, reach, skew, False)
    places = jnp.arange(count)

    def named(lengths, offset_by):
        used = int((lengths > 0).sum())
        fixed = max(1, used // 4)
        moved = fixed + (places - fixed + offset_by * (used - fixed)) % max(1, count - fixed)
        return jnp.zeros((count,), jnp.int32).at[sequence[jnp.where(places < fixed, places, moved)]].set(jnp.asarray(lengths, jnp.int32))

    lengths = jnp.where(number % 4 == 0, named(crowded, number // 4), named(usual, number - number // 4 - 1))
    mixed = jax.random.permutation(jax.random.fold_in(own, 3), count)
    source_of, receiver = mixed[0:count // 2 * 2:2], mixed[1:count // 2 * 2:2]
    margin = jnp.minimum(lengths[source_of] - 1, reach - lengths[receiver]) // 2
    margin = jnp.where((source_of == sequence[0]) | (receiver == sequence[0]) | (lengths[receiver] == 0), 0, jnp.maximum(margin, 0))
    moved = jax.random.randint(jax.random.fold_in(own, 4), (count // 2,), 0, 1 << 20) % (margin + 1)
    lengths = lengths.at[source_of].add(-moved).at[receiver].add(moved)
    items = jnp.searchsorted(jnp.cumsum(lengths), jnp.arange(rows * top), side="right").astype(jnp.int32)
    table = items.reshape(top, rows).T
    table = table[jax.random.permutation(jax.random.fold_in(own, 1), rows)]
    offset_by = jax.random.randint(jax.random.fold_in(own, 2), (rows, 1), 0, top)
    return jnp.take_along_axis(table, (jnp.arange(top)[None, :] + offset_by) % top, axis=1)


def shares(count, total, limit, lean, full):
    loads = [(1 << 20) // math.isqrt(grade ** lean) + 1 for grade in range(1, count + 1)]
    largest = limit if full else min(limit, max(-(-total // count), total * loads[0] // sum(loads)))
    least = 1 if total - largest >= count - 1 else 0
    holding, rest = [largest] + [least] * (count - 1), total - largest - least * (count - 1)
    while rest > 0:
        free = [i for i in range(1, count) if holding[i] < largest] or [i for i in range(1, count) if holding[i] < limit]
        whole, left = sum([loads[i] for i in free]), rest
        for i in free:
            addition = min(limit - holding[i], max(1, left * loads[i] // whole), rest)
            holding[i] = holding[i] + addition
            rest = rest - addition
    return np.array(holding)


def bell_draw(key, dims, deviation, most, shards=(), kind=jnp.bfloat16):
    level = block_levels(key, dims, shards, -0.22, 0.18) if shards else 1.0
    drawn = jax.random.normal(key, dims, jnp.float32) * deviation * level
    return jnp.minimum(jnp.maximum(drawn, -most), most).astype(kind)


def setup_inputs(seed: int = 0) -> dict:
    key_of = jax.random.split(jax.random.key(seed), 14)
    inputs = bell_draw(key_of[0], (MICRO, BATCH, SEQ, MODEL_DIMENSION), 1.0, 6.0, ((1, 16),))
    cotangent = bell_draw(key_of[1], (MICRO, BATCH, SEQ, MODEL_DIMENSION), 1.0, 6.0, ((1, 16),))
    segments = jax.vmap(lambda own: jnp.searchsorted(jnp.cumsum(ragged(own, SEGS, SEQ, SEQ // 2, 1)), jnp.arange(SEQ), side="right"))(jax.random.split(key_of[2], MICRO * BATCH)).reshape((MICRO, BATCH, SEQ)).astype(jnp.int32)
    routes_keys = jax.random.split(jax.random.fold_in(key_of[3], 1), LAYER_COUNT * MICRO * BATCH * SEQ // SEQ)
    routes_turns = jax.random.permutation(jax.random.fold_in(key_of[3], 3), LAYER_COUNT * MICRO * BATCH * SEQ // SEQ)
    routes = jax.vmap(lambda own, number: deal_out(jax.random.fold_in(key_of[3], 2), own, number, SEQ, EXPERTS, TOP, CAP, 1))(routes_keys, routes_turns).reshape((LAYER_COUNT, MICRO, BATCH, SEQ, TOP))
    norm_attn = jnp.clip(1.0 + 0.1 * jax.random.normal(key_of[4], (LAYER_COUNT, MODEL_DIMENSION), jnp.float32), 0.5, 1.5)
    w_query = bell_draw(key_of[5], (LAYER_COUNT, MODEL_DIMENSION, QUERY_HEADS * HEAD_DIMENSION), MODEL_DIMENSION ** -0.5, 0.1875, ((0, 2), (1, 4)))
    key_value_weight = bell_draw(key_of[6], (LAYER_COUNT, MODEL_DIMENSION, 2 * KEY_VALUE_HEADS * HEAD_DIMENSION), MODEL_DIMENSION ** -0.5, 0.1875, ((0, 2), (1, 4)))
    w_out = bell_draw(key_of[7], (LAYER_COUNT, QUERY_HEADS * HEAD_DIMENSION, MODEL_DIMENSION), (QUERY_HEADS * HEAD_DIMENSION * 4 // SEQ) ** -0.5, 0.75, ((0, 2), (1, 4)))
    norm_ffn = jnp.clip(1.0 + 0.1 * jax.random.normal(key_of[8], (LAYER_COUNT, MODEL_DIMENSION), jnp.float32), 0.5, 1.5)
    w_router = bell_draw(key_of[9], (LAYER_COUNT, MODEL_DIMENSION, EXPERTS), (4 * MODEL_DIMENSION) ** -0.5, 0.09375, ((0, 2),))
    w_gate = bell_draw(key_of[10], (LAYER_COUNT, EXPERTS, MODEL_DIMENSION, FF), MODEL_DIMENSION ** -0.5, 0.1875, ((0, 2), (1, 4)))
    w_up = bell_draw(key_of[11], (LAYER_COUNT, EXPERTS, MODEL_DIMENSION, FF), MODEL_DIMENSION ** -0.5, 0.1875, ((0, 2), (1, 4)))
    w_down = bell_draw(key_of[12], (LAYER_COUNT, EXPERTS, FF, MODEL_DIMENSION), (FF // 16) ** -0.5, 1.0, ((0, 2), (1, 4)))
    return dict(inputs=inputs, cotangent=cotangent, segments=segments, routes=routes, norm_attn=norm_attn, w_query=w_query, key_value_weight=key_value_weight, w_out=w_out, norm_ffn=norm_ffn, w_router=w_router, w_gate=w_gate, w_up=w_up, w_down=w_down)


@jax.custom_vjp
def lowered_input(v):
    return lax.optimization_barrier(v.astype(jnp.bfloat16)).astype(jnp.float32)

@jax.custom_vjp
def low_back(v):
    return v

def low_keep(v):
    return (lowered_input(v), None)

def low_pass(kept, grad):
    return (grad,)

def back_keep(v):
    return (v, None)

def back_low(kept, grad):
    return (lowered_input(grad),)
lowered_input.defvjp(low_keep, low_pass)
low_back.defvjp(back_keep, back_low)
epsilon = 1e-06
rope_base = 10000.0
highest = lax.Precision.HIGHEST

def normed(values_in, gain_vec):
    return values_in * lax.rsqrt(lax.optimization_barrier(jnp.mean(values_in * values_in, axis=-1, keepdims=True)) + epsilon) * gain_vec

def rotary_embed(values_in, token_position):
    half_dim = values_in.shape[-1] // 2
    frequency = rope_base ** (-jnp.arange(half_dim, dtype=jnp.float32) / half_dim)
    angles = token_position.astype(jnp.float32)[..., None, None] * frequency
    cosine = jnp.cos(angles)
    sine_part = jnp.sin(angles)
    leading = values_in[..., :half_dim]
    trailing = values_in[..., half_dim:]
    return jnp.concatenate([leading * cosine - trailing * sine_part, trailing * cosine + leading * sine_part], axis=-1)

def positions(segment):
    earlier = lax.optimization_barrier(jnp.sum((segment[..., None, :] < segment[..., :, None]).astype(jnp.int32), axis=-1))
    return jnp.arange(segment.shape[-1], dtype=jnp.int32) - earlier

def causal(segment):
    order_idx = jnp.arange(segment.shape[-1], dtype=jnp.int32)
    return (segment[..., :, None] == segment[..., None, :]) & (order_idx[None, :] <= order_idx[:, None])

def places(routing):
    flat_ids = routing.reshape(routing.shape[:-2] + (-1,))
    onehot = (flat_ids[..., None] == jnp.arange(EXPERTS, dtype=jnp.int32)).astype(jnp.int32)
    earlier_count = jnp.cumsum(onehot, axis=-2) - onehot
    return (flat_ids * CAP + lax.optimization_barrier(jnp.sum(earlier_count * onehot, axis=-1))).astype(jnp.int32)

def attend(query_matrix, key_matrix, value_matrix, segment):
    batch_list, sequence_length = (query_matrix.shape[0], query_matrix.shape[1])
    grouped_queries = query_matrix.reshape(batch_list, sequence_length, KEY_VALUE_HEADS, QUERY_HEADS // KEY_VALUE_HEADS, HEAD_DIMENSION)
    scores = low_back(jnp.einsum('bqhgd,bkhd->bhgqk', grouped_queries, key_matrix, precision=highest) * HEAD_DIMENSION ** (-0.5))
    allowed = causal(segment)[:, None, None]
    scores = jnp.where(allowed, scores, -1e+30)
    attend_weights = lowered_input(jax.nn.softmax(scores, axis=-1))
    attended = jnp.einsum('bhgqk,bkhd->bqhgd', attend_weights, value_matrix, precision=highest)
    return attended.reshape(batch_list, sequence_length, QUERY_HEADS * HEAD_DIMENSION)

def expert_rows(slot_rows, gate_w, up_w, down_w):
    gate_lin = low_back(jnp.dot(slot_rows, gate_w, precision=highest))
    up_lin = low_back(jnp.dot(slot_rows, up_w, precision=highest))
    inner_act = lowered_input(jax.nn.silu(gate_lin) * up_lin)
    return lowered_input(low_back(jnp.dot(inner_act, down_w, precision=highest)))

def mixture(ffn_normed, gates, routing, gate_w, up_w, down_w):
    micro_batches, batch_list, sequence_length, model_width = ffn_normed.shape
    slot_place = places(routing)
    tokens = jnp.broadcast_to(jnp.arange(sequence_length * TOP, dtype=jnp.int32) // TOP, slot_place.shape)
    leading = jnp.arange(micro_batches, dtype=jnp.int32)[:, None, None]
    second_idx = jnp.arange(batch_list, dtype=jnp.int32)[None, :, None]
    slot_table = jnp.full((micro_batches, batch_list, EXPERTS * CAP), sequence_length, jnp.int32)
    slot_table = slot_table.at[leading, second_idx, slot_place].set(tokens)
    padded = jnp.concatenate([ffn_normed, jnp.zeros((micro_batches, batch_list, 1, model_width), jnp.float32)], axis=2)
    slot_rows = low_back(padded[leading, second_idx, slot_table])
    slot_rows = slot_rows.reshape(micro_batches * batch_list, EXPERTS, CAP, model_width).transpose(1, 0, 2, 3)
    slot_rows = slot_rows.reshape(EXPERTS, micro_batches * batch_list * CAP, model_width)
    results = lax.map(jax.checkpoint(lambda packed: expert_rows(*packed)), (slot_rows, gate_w, up_w, down_w))
    results = results.reshape(EXPERTS, micro_batches * batch_list, CAP, model_width).transpose(1, 0, 2, 3)
    results = results.reshape(micro_batches, batch_list, EXPERTS * CAP, model_width)
    picked = results[leading, second_idx, slot_place].reshape(micro_batches, batch_list, sequence_length, TOP, model_width)
    return jnp.einsum('mbsk,mbskd->mbsd', gates, picked, precision=highest)

def block_layer(stream, gain_attn, w_query, key_value_weight, w_out, gain_ffn, w_router, w_gate, w_up, w_down, segments, routing):
    micro_batches, batch_list, sequence_length, model_width = stream.shape
    attn_normed = lowered_input(normed(stream, gain_attn))
    query_lin = low_back(jnp.einsum('mbsd,de->mbse', attn_normed, w_query, precision=highest))
    key_value_linear = low_back(jnp.einsum('mbsd,de->mbse', attn_normed, key_value_weight, precision=highest))
    token_position = positions(segments)
    split_index = KEY_VALUE_HEADS * HEAD_DIMENSION
    query_matrix = lowered_input(rotary_embed(query_lin.reshape(micro_batches, batch_list, sequence_length, QUERY_HEADS, HEAD_DIMENSION), token_position))
    key_matrix = lowered_input(rotary_embed(key_value_linear[..., :split_index].reshape(micro_batches, batch_list, sequence_length, KEY_VALUE_HEADS, HEAD_DIMENSION), token_position))
    value_matrix = lowered_input(key_value_linear[..., split_index:].reshape(micro_batches, batch_list, sequence_length, KEY_VALUE_HEADS, HEAD_DIMENSION))
    attended = lax.map(jax.checkpoint(lambda packed: attend(*packed)), (query_matrix, key_matrix, value_matrix, segments))
    attended = lowered_input(low_back(attended))
    middle = stream + low_back(jnp.einsum('mbse,ed->mbsd', attended, w_out, precision=highest))
    ffn_normed = lowered_input(normed(middle, gain_ffn))
    logits = jnp.einsum('mbsd,de->mbse', ffn_normed, w_router, precision=highest)
    gates = jax.nn.softmax(jnp.take_along_axis(logits, routing, axis=-1), axis=-1)
    return middle + mixture(ffn_normed, gates, routing, w_gate, w_up, w_down)

def reference(inputs, cotangent, segments, routes, norm_attn, w_query, key_value_weight, w_out, norm_ffn, w_router, w_gate, w_up, w_down):
    current = inputs.astype(jnp.float32)
    outs_list = []
    pullbacks = []
    for layer_idx in range(LAYER_COUNT):
        weights_now = (norm_attn[layer_idx], w_query[layer_idx].astype(jnp.float32), key_value_weight[layer_idx].astype(jnp.float32), w_out[layer_idx].astype(jnp.float32), norm_ffn[layer_idx], w_router[layer_idx].astype(jnp.float32), w_gate[layer_idx].astype(jnp.float32), w_up[layer_idx].astype(jnp.float32), w_down[layer_idx].astype(jnp.float32))

        def section_fn(stream, *weight_list, layer_idx=layer_idx):
            return block_layer(stream, *weight_list, segments, routes[layer_idx])
        current, pullback = jax.vjp(section_fn, current, *weights_now)
        outs_list.append(current)
        pullbacks.append(pullback)
    carried = cotangent.astype(jnp.float32)
    collected = [None] * LAYER_COUNT
    for layer_idx in reversed(range(LAYER_COUNT)):
        pieces = pullbacks[layer_idx](carried)
        carried = pieces[0]
        collected[layer_idx] = pieces
    stacked = [jnp.stack([pieces[member] for pieces in collected]) for member in range(10)]
    hidden = jnp.stack(outs_list)
    return (hidden, stacked[0], stacked[1], stacked[2], stacked[3], stacked[4], stacked[5], stacked[6], stacked[7], stacked[8], stacked[9])
```

```python
import jax
import jax.numpy as jnp
from jax import lax
from jax.sharding import PartitionSpec as P

QUERY_HEADS = 16
KEY_VALUE_HEADS = 8
HEAD_DIMENSION = 64
EXPERTS = 32


epsilon = 1e-06
rope_base = 10000.0
highest = lax.Precision.HIGHEST


def normed(values_in, gain_vec):
    return (
        values_in
        * lax.rsqrt(jnp.mean(values_in * values_in, axis=-1, keepdims=True) + epsilon)
        * gain_vec
    )


def rotary_embed(values_in, token_position):
    half_dim = values_in.shape[-1] // 2
    frequency = rope_base ** (-jnp.arange(half_dim, dtype=jnp.float32) / half_dim)
    angles = token_position.astype(jnp.float32)[..., None, None] * frequency
    cosine = jnp.cos(angles)
    sine_part = jnp.sin(angles)
    leading = values_in[..., :half_dim]
    trailing = values_in[..., half_dim:]
    return jnp.concatenate(
        [leading * cosine - trailing * sine_part, trailing * cosine + leading * sine_part], axis=-1
    )


def positions(segment):
    earlier = jnp.sum((segment[..., None, :] < segment[..., :, None]).astype(jnp.int32), axis=-1)
    return jnp.arange(segment.shape[-1], dtype=jnp.int32) - earlier


def causal(segment):
    order_idx = jnp.arange(segment.shape[-1], dtype=jnp.int32)
    return (segment[..., :, None] == segment[..., None, :]) & (
        order_idx[None, :] <= order_idx[:, None]
    )


def attention_scores(query_matrix, key_matrix, allowed):
    sequence_length = query_matrix.shape[0]
    grouped_queries = query_matrix.reshape(
        sequence_length, KEY_VALUE_HEADS, QUERY_HEADS // KEY_VALUE_HEADS, HEAD_DIMENSION
    )
    scores = jnp.einsum(
        "qhgd,khd->hgqk", grouped_queries, key_matrix, preferred_element_type=jnp.float32
    ) * HEAD_DIMENSION ** (-0.5)
    return jnp.where(allowed[None, None], scores, -1e30)


everyone = ("dp", "expert")


def both_layers(block):
    return lax.all_gather(block, "pipe", axis=0, tiled=False)


def rows_of_all(block):
    return lax.all_gather(block, everyone, axis=0, tiled=True)


def summed_rows(block):
    return lax.psum_scatter(block, everyone, scatter_dimension=0, tiled=True)


def dot32(left, right):
    return jnp.dot(left, right, preferred_element_type=jnp.float32)


def expand_matrix(local_experts, slice_width, first_expert):
    column = jnp.arange(4 * EXPERTS)[:, None]
    owner = first_expert + jnp.arange(local_experts * slice_width)[None, :] // slice_width
    return ((column % EXPERTS == owner) & (column < 2 * EXPERTS)).astype(jnp.bfloat16)


def collect_matrix(local_experts, slice_width, first_expert, part, parts):
    column = jnp.arange(parts * EXPERTS)[None, :]
    owner = first_expert + jnp.arange(local_experts * slice_width)[:, None] // slice_width
    return (column == part * EXPERTS + owner).astype(jnp.float32)


def forward_layer(stream, segment, routing, attention, gains, router, experts, expand):
    full_query_keyval, full_out = attention
    gain_attn, gain_ffn = gains
    gate_w, up_w, down_w = experts
    sequence_length, model_width = stream.shape
    attn_normed = normed(stream, gain_attn).astype(jnp.bfloat16)
    query_width = QUERY_HEADS * HEAD_DIMENSION
    split_index = KEY_VALUE_HEADS * HEAD_DIMENSION
    linear = dot32(attn_normed, full_query_keyval)
    query_lin = linear[:, :query_width]
    key_value_linear = linear[:, query_width:]
    token_position = positions(segment)
    query_matrix = rotary_embed(
        query_lin.reshape(sequence_length, QUERY_HEADS, HEAD_DIMENSION), token_position
    ).astype(jnp.bfloat16)
    key_matrix = rotary_embed(
        key_value_linear[:, :split_index].reshape(sequence_length, KEY_VALUE_HEADS, HEAD_DIMENSION),
        token_position,
    ).astype(jnp.bfloat16)
    value_matrix = (
        key_value_linear[:, split_index:]
        .reshape(sequence_length, KEY_VALUE_HEADS, HEAD_DIMENSION)
        .astype(jnp.bfloat16)
    )
    scores = attention_scores(query_matrix, key_matrix, causal(segment))
    row_peak = jnp.max(scores, axis=-1, keepdims=True)
    exponent = jnp.exp(scores - row_peak)
    totals = jnp.sum(exponent, axis=-1, keepdims=True)
    attend_prob = exponent / totals
    attended = jnp.einsum(
        "hgqk,khd->qhgd",
        attend_prob.astype(jnp.bfloat16),
        value_matrix,
        preferred_element_type=jnp.float32,
    )
    attended = attended.reshape(sequence_length, QUERY_HEADS * HEAD_DIMENSION).astype(jnp.bfloat16)
    middle = stream + dot32(attended, full_out)
    ffn_normed = normed(middle, gain_ffn).astype(jnp.bfloat16)
    logits = dot32(ffn_normed, router)
    choose = (routing[:, :, None] == jnp.arange(EXPERTS, dtype=jnp.int32)).astype(jnp.float32)
    gates = jax.nn.softmax(jnp.sum(choose * logits[:, None, :], axis=-1), axis=-1)
    gate_matrix = jnp.sum(choose * gates[:, :, None], axis=1)
    gate_high = lax.reduce_precision(gate_matrix, 8, 7)
    gate_rest = gate_matrix - gate_high
    sent = jnp.concatenate(
        [
            ffn_normed,
            gate_high.astype(jnp.bfloat16),
            gate_rest.astype(jnp.bfloat16),
            jnp.zeros((sequence_length, 2 * EXPERTS), jnp.bfloat16),
        ],
        axis=1,
    )
    arrived = rows_of_all(sent)
    token_rows = arrived[:, :model_width]
    spread_gates = dot32(arrived[:, model_width:], expand)
    gate_lin = dot32(token_rows, gate_w)
    up_lin = dot32(token_rows, up_w)
    inner_act = (jax.nn.silu(gate_lin) * up_lin).astype(jnp.bfloat16)
    weighted = (inner_act.astype(jnp.float32) * spread_gates).astype(jnp.bfloat16)
    mixture = summed_rows(dot32(weighted, down_w).astype(jnp.bfloat16))
    retained = (
        stream,
        attn_normed,
        query_matrix,
        key_matrix,
        value_matrix,
        attend_prob,
        attended,
        middle,
        ffn_normed,
        choose,
        gates,
        token_rows,
        spread_gates,
        gate_lin,
        up_lin,
        inner_act,
        weighted,
    )
    return (middle + mixture.astype(jnp.float32), retained)


def backward_layer(
    carried, retained, segment, attention, gains, router, experts, collect
):
    full_query_keyval, full_out = attention
    gain_attn, gain_ffn = gains
    gate_w, up_w, down_w = experts
    (
        stream,
        attn_normed,
        query_matrix,
        key_matrix,
        value_matrix,
        attend_prob,
        attended,
        middle,
        ffn_normed,
        choose,
        gates,
        token_rows,
        spread_gates,
        gate_lin,
        up_lin,
        inner_act,
        weighted,
    ) = retained
    sequence_length, model_width = carried.shape
    carried_rows = rows_of_all(carried.astype(jnp.bfloat16))
    plain_grad = jnp.einsum("td,fd->tf", carried_rows, down_w, preferred_element_type=jnp.float32)
    choice_grads = jnp.dot(
        inner_act.astype(jnp.float32) * plain_grad, collect, precision=highest
    )
    inner_grad = spread_gates * plain_grad
    squashed = jax.nn.sigmoid(gate_lin)
    gate_low = (inner_grad * up_lin * squashed * (1.0 + gate_lin * (1.0 - squashed))).astype(
        jnp.bfloat16
    )
    up_low = (inner_grad * gate_lin * squashed).astype(jnp.bfloat16)
    row_grads = jnp.einsum("tf,df->td", gate_low, gate_w, preferred_element_type=jnp.float32)
    row_grads = row_grads + jnp.einsum(
        "tf,df->td", up_low, up_w, preferred_element_type=jnp.float32
    )
    returned = summed_rows(
        jnp.concatenate(
            [row_grads.astype(jnp.bfloat16), choice_grads.astype(jnp.bfloat16)], axis=1
        )
    ).astype(jnp.float32)
    expert_grads = (
        jnp.einsum("td,tf->df", token_rows, gate_low, preferred_element_type=jnp.float32),
        jnp.einsum("td,tf->df", token_rows, up_low, preferred_element_type=jnp.float32),
        jnp.einsum("tf,td->fd", weighted, carried_rows, preferred_element_type=jnp.float32),
    )
    expert_grads = tuple(grad.astype(jnp.bfloat16) for grad in expert_grads)
    all_choices = jnp.sum(
        returned[:, model_width:].reshape(sequence_length, -1, EXPERTS), axis=1
    )
    gate_grad = jnp.sum(choose * all_choices[:, None, :], axis=-1)
    chosen_grad = gates * (gate_grad - jnp.sum(gates * gate_grad, axis=-1, keepdims=True))
    logit_grad = jnp.sum(choose * chosen_grad[:, :, None], axis=1)
    router_grad = jnp.einsum(
        "sd,se->de", ffn_normed.astype(jnp.float32), logit_grad, precision=highest
    )
    ffn_grad = jnp.einsum("se,de->sd", logit_grad, router.astype(jnp.float32), precision=highest)
    ffn_grad = ffn_grad + returned[:, :model_width]
    middle_grad, gain_ffn_grad = jax.vjp(normed, middle, gain_ffn)[1](ffn_grad)
    middle_grad = middle_grad + carried
    branch_grad = middle_grad.astype(jnp.bfloat16)
    attention_output_grad = jnp.einsum(
        "sd,ed->se", branch_grad, full_out, preferred_element_type=jnp.float32
    ).astype(jnp.bfloat16)
    query_group_size = QUERY_HEADS // KEY_VALUE_HEADS
    grouped_gradient = attention_output_grad.reshape(
        sequence_length, KEY_VALUE_HEADS, query_group_size, HEAD_DIMENSION
    )
    prob_grad = jnp.einsum(
        "qhgd,khd->hgqk", grouped_gradient, value_matrix, preferred_element_type=jnp.float32
    )
    score_grad = (
        attend_prob * (prob_grad - jnp.sum(prob_grad * attend_prob, axis=-1, keepdims=True))
    ).astype(jnp.bfloat16)
    grouped_queries = query_matrix.reshape(
        sequence_length, KEY_VALUE_HEADS, query_group_size, HEAD_DIMENSION
    )
    query_grad = jnp.einsum(
        "hgqk,khd->qhgd", score_grad, key_matrix, preferred_element_type=jnp.float32
    ).reshape(sequence_length, QUERY_HEADS, HEAD_DIMENSION) * HEAD_DIMENSION ** (-0.5)
    key_gradient = jnp.einsum(
        "hgqk,qhgd->khd", score_grad, grouped_queries, preferred_element_type=jnp.float32
    ) * HEAD_DIMENSION ** (-0.5)
    value_gradient = jnp.einsum(
        "hgqk,qhgd->khd",
        attend_prob.astype(jnp.bfloat16),
        grouped_gradient,
        preferred_element_type=jnp.float32,
    )
    back_position = -positions(segment)
    lows = jnp.concatenate(
        [
            rotary_embed(query_grad, back_position).reshape(sequence_length, -1),
            rotary_embed(key_gradient, back_position).reshape(sequence_length, -1),
            value_gradient.reshape(sequence_length, -1),
        ],
        axis=1,
    ).astype(jnp.bfloat16)
    normed_grad = jnp.einsum(
        "se,de->sd", lows, full_query_keyval, preferred_element_type=jnp.float32
    )
    stream_grad, gain_attn_grad = jax.vjp(normed, stream, gain_attn)[1](normed_grad)
    shared = jnp.concatenate(
        [
            jnp.einsum("sd,se->de", attn_normed, lows, preferred_element_type=jnp.float32),
            jnp.einsum("se,sd->ed", attended, branch_grad, preferred_element_type=jnp.float32),
            router_grad,
            gain_attn_grad[:, None],
            gain_ffn_grad[:, None],
            jnp.zeros((model_width, 128 - EXPERTS - 2), jnp.float32),
        ],
        axis=1,
    ).astype(jnp.bfloat16)
    return (stream_grad + middle_grad, shared, expert_grads)


def on_device(
    inputs,
    cotangent,
    segments,
    routes,
    norm_attn,
    w_query,
    key_value_weight,
    w_out,
    norm_ffn,
    w_router,
    w_gate,
    w_up,
    w_down,
):
    layers = lax.axis_size("pipe")
    core = lax.axis_index("pipe")
    part = lax.axis_index("dp")
    parts = lax.axis_size("dp")
    local_experts, model_width, hidden_units = w_gate.shape[1:]
    slice_width = hidden_units // parts
    first_expert = lax.axis_index("expert") * local_experts

    def own(block, axis=0):
        return lax.dynamic_index_in_dim(block, core, axis, keepdims=False)

    stream = own(inputs)[0].astype(jnp.float32)
    carried = own(cotangent)[0].astype(jnp.float32)
    segment = own(segments)[0]
    routing = own(both_layers(routes[0]), 1)[:, 0]
    gains = both_layers(jnp.concatenate([norm_attn, norm_ffn], axis=0))
    router = both_layers(w_router[0])
    query_keyval = both_layers(
        lax.all_gather(
            jnp.concatenate([w_query[0], key_value_weight[0]], axis=1), "dp", axis=0, tiled=True
        )
    )
    out_full = both_layers(lax.all_gather(w_out[0], "dp", axis=0, tiled=True))

    def columns(weight):
        piece = lax.dynamic_slice_in_dim(weight[0], part * slice_width, slice_width, 2)
        return piece.transpose(1, 0, 2).reshape(model_width, local_experts * slice_width)

    down_piece = lax.dynamic_slice_in_dim(w_down[0], part * slice_width, slice_width, 1)
    gate_all = both_layers(columns(w_gate))
    up_all = both_layers(columns(w_up))
    down_all = both_layers(down_piece.reshape(local_experts * slice_width, model_width))
    expand = expand_matrix(local_experts, slice_width, first_expert)
    collect = collect_matrix(local_experts, slice_width, first_expert, part, parts)

    def params(layer):
        return (
            (query_keyval[layer], out_full[layer]),
            (gains[layer, 0], gains[layer, 1]),
            router[layer],
            (gate_all[layer], up_all[layer], down_all[layer]),
        )

    results, kept = [], []
    for layer in range(layers):
        stream, retained = forward_layer(stream, segment, routing[layer], *params(layer), expand)
        results.append(stream)
        kept.append(retained)
    grads_in, totals = [None] * layers, [None] * layers
    for layer in reversed(range(layers)):
        carried, shared, expert_grads = backward_layer(
            carried, kept[layer], segment, *params(layer), collect
        )
        grads_in[layer] = carried
        leaves = (shared,) + expert_grads
        totals[layer] = [
            leaf.astype(jnp.float32)
            + lax.ppermute(
                leaf, "pipe", [(other, layer) for other in range(layers) if other != layer]
            ).astype(jnp.float32)
            for leaf in leaves
        ]
    shared, gate_grad, up_grad, down_grad = [
        jnp.where(core == 0, first, second) for first, second in zip(*totals)
    ]
    shared = lax.psum_scatter(
        shared.astype(jnp.bfloat16), "dp", scatter_dimension=0, tiled=True
    )
    shared = lax.psum(shared, "expert").astype(jnp.float32)

    def swap(first, second):
        ours = jnp.where(core == 0, first, second)
        theirs = lax.ppermute(
            jnp.where(core == 0, second, first).astype(jnp.bfloat16), "pipe", [(0, 1), (1, 0)]
        ).astype(jnp.float32)
        return jnp.stack(
            [jnp.where(core == 0, ours, theirs), jnp.where(core == 0, theirs, ours)]
        )

    def expert_layout(grad):
        return grad.reshape(model_width, local_experts, slice_width).transpose(1, 0, 2)[None]

    width = model_width
    return (
        swap(*results)[None, :, None],
        swap(*grads_in)[None, :, None],
        shared[None, :, 3 * width + EXPERTS],
        shared[None, :, :width],
        shared[None, :, width : 2 * width],
        shared[None, :, 2 * width : 3 * width],
        shared[None, :, 3 * width + EXPERTS + 1],
        shared[None, :, 3 * width : 3 * width + EXPERTS],
        expert_layout(gate_grad),
        expert_layout(up_grad),
        down_grad.reshape(1, local_experts, slice_width, model_width),
    )


def solution(mesh):
    return jax.shard_map(
        on_device,
        mesh=mesh,
        in_specs=(
            P(None, ("dp", "expert"), None, None),
            P(None, ("dp", "expert"), None, None),
            P(None, ("dp", "expert"), None),
            P("pipe", None, ("dp", "expert"), None, None),
            P("pipe", None),
            P("pipe", "dp", None),
            P("pipe", "dp", None),
            P("pipe", "dp", None),
            P("pipe", None),
            P("pipe", None, None),
            P("pipe", "expert", None, None),
            P("pipe", "expert", None, None),
            P("pipe", "expert", None, None),
        ),
        out_specs=(
            P("pipe", None, ("dp", "expert"), None, None),
            P("pipe", None, ("dp", "expert"), None, None),
            P("pipe", "dp"),
            P("pipe", "dp", None),
            P("pipe", "dp", None),
            P("pipe", "dp", None),
            P("pipe", "dp"),
            P("pipe", "dp", None),
            P("pipe", "expert", None, "dp"),
            P("pipe", "expert", None, "dp"),
            P("pipe", "expert", "dp", None),
        ),
        check_vma=False,
    )
```

```python
import jax
import jax.numpy as jnp
from jax import lax
from jax.sharding import PartitionSpec as P

QUERY_HEADS = 16
KEY_VALUE_HEADS = 8
HEAD_DIMENSION = 64
EXPERTS = 32


epsilon = 1e-06
rope_base = 10000.0
highest = lax.Precision.HIGHEST


def normed(values_in, gain_vec):
    return (
        values_in
        * lax.rsqrt(jnp.mean(values_in * values_in, axis=-1, keepdims=True) + epsilon)
        * gain_vec
    )


def rotary_embed(values_in, token_position):
    half_dim = values_in.shape[-1] // 2
    frequency = rope_base ** (-jnp.arange(half_dim, dtype=jnp.float32) / half_dim)
    angles = token_position.astype(jnp.float32)[..., None, None] * frequency
    cosine = jnp.cos(angles)
    sine_part = jnp.sin(angles)
    leading = values_in[..., :half_dim]
    trailing = values_in[..., half_dim:]
    return jnp.concatenate(
        [leading * cosine - trailing * sine_part, trailing * cosine + leading * sine_part], axis=-1
    )


def positions(segment):
    earlier = jnp.sum((segment[..., None, :] < segment[..., :, None]).astype(jnp.int32), axis=-1)
    return jnp.arange(segment.shape[-1], dtype=jnp.int32) - earlier


def causal(segment):
    order_idx = jnp.arange(segment.shape[-1], dtype=jnp.int32)
    return (segment[..., :, None] == segment[..., None, :]) & (
        order_idx[None, :] <= order_idx[:, None]
    )


def attention_scores(query_matrix, key_matrix, allowed):
    sequence_length = query_matrix.shape[0]
    grouped_queries = query_matrix.reshape(
        sequence_length, KEY_VALUE_HEADS, QUERY_HEADS // KEY_VALUE_HEADS, HEAD_DIMENSION
    )
    scores = jnp.einsum(
        "qhgd,khd->hgqk", grouped_queries, key_matrix, preferred_element_type=jnp.float32
    ) * HEAD_DIMENSION ** (-0.5)
    return jnp.where(allowed[None, None], scores, -1e30)


def both_layers(block):
    return lax.all_gather(block, "pipe", axis=0, tiled=False)


def layer_pair(block):
    other = lax.ppermute(block, "pipe", [(0, 1), (1, 0)])
    first = lax.axis_index("pipe") == 0
    return jnp.where(first, block, other), jnp.where(first, other, block)


def ahead(axis, step):
    count = lax.axis_size(axis)
    return [(i, (i + step) % count) for i in range(count)]


def across(axis, step):
    return [(i, i ^ step) for i in range(lax.axis_size(axis))]


def rows_of_all(block):
    blocks = [block]
    for step in range(1, lax.axis_size("expert")):
        blocks.append(lax.ppermute(block, "expert", ahead("expert", step)))
    block = jnp.concatenate(blocks, axis=0)
    blocks = [block]
    for step in range(1, lax.axis_size("dp")):
        blocks.append(lax.ppermute(block, "dp", across("dp", step)))
    return jnp.concatenate(blocks, axis=0)


def summed_rows(block):
    blocks = jnp.split(block, lax.axis_size("dp"), axis=0)
    total = blocks[0].astype(jnp.float32)
    for step in range(1, len(blocks)):
        total = total + lax.ppermute(blocks[step], "dp", across("dp", step)).astype(jnp.float32)
    blocks = jnp.split(total.astype(jnp.bfloat16), lax.axis_size("expert"), axis=0)
    total = blocks[0].astype(jnp.float32)
    for step in range(1, len(blocks)):
        arrived = lax.ppermute(blocks[step], "expert", ahead("expert", -step))
        total = total + arrived.astype(jnp.float32)
    return total


def dot32(left, right):
    return jnp.dot(left, right, preferred_element_type=jnp.float32)


def expand_matrix(local_experts, slice_width, first_expert):
    column = jnp.arange(4 * EXPERTS)[:, None]
    owner = first_expert + jnp.arange(local_experts * slice_width)[None, :] // slice_width
    return ((column % EXPERTS == owner) & (column < 2 * EXPERTS)).astype(jnp.bfloat16)


def collect_matrix(local_experts, slice_width, first_expert, part, parts):
    column = jnp.arange(parts * EXPERTS)[None, :]
    owner = first_expert + jnp.arange(local_experts * slice_width)[:, None] // slice_width
    return (column == part * EXPERTS + owner).astype(jnp.float32)


def forward_layer(stream, segment, routing, attention, gains, router, experts, expand):
    full_query_keyval, full_out = attention
    gain_attn, gain_ffn = gains
    gate_w, up_w, down_w = experts
    sequence_length, model_width = stream.shape
    attn_normed = normed(stream, gain_attn).astype(jnp.bfloat16)
    query_width = QUERY_HEADS * HEAD_DIMENSION
    split_index = KEY_VALUE_HEADS * HEAD_DIMENSION
    linear = dot32(attn_normed, full_query_keyval)
    query_lin = linear[:, :query_width]
    key_value_linear = linear[:, query_width:]
    token_position = positions(segment)
    query_matrix = rotary_embed(
        query_lin.reshape(sequence_length, QUERY_HEADS, HEAD_DIMENSION), token_position
    ).astype(jnp.bfloat16)
    key_matrix = rotary_embed(
        key_value_linear[:, :split_index].reshape(sequence_length, KEY_VALUE_HEADS, HEAD_DIMENSION),
        token_position,
    ).astype(jnp.bfloat16)
    value_matrix = (
        key_value_linear[:, split_index:]
        .reshape(sequence_length, KEY_VALUE_HEADS, HEAD_DIMENSION)
        .astype(jnp.bfloat16)
    )
    scores = attention_scores(query_matrix, key_matrix, causal(segment))
    row_peak = jnp.max(scores, axis=-1, keepdims=True)
    exponent = jnp.exp(scores - row_peak)
    totals = jnp.sum(exponent, axis=-1, keepdims=True)
    attend_prob = exponent / totals
    attended = jnp.einsum(
        "hgqk,khd->qhgd",
        attend_prob.astype(jnp.bfloat16),
        value_matrix,
        preferred_element_type=jnp.float32,
    )
    attended = attended.reshape(sequence_length, QUERY_HEADS * HEAD_DIMENSION).astype(jnp.bfloat16)
    middle = stream + dot32(attended, full_out)
    ffn_normed = normed(middle, gain_ffn).astype(jnp.bfloat16)
    logits = dot32(ffn_normed, router)
    choose = (routing[:, :, None] == jnp.arange(EXPERTS, dtype=jnp.int32)).astype(jnp.float32)
    gates = jax.nn.softmax(jnp.sum(choose * logits[:, None, :], axis=-1), axis=-1)
    gate_matrix = jnp.sum(choose * gates[:, :, None], axis=1)
    gate_high = lax.reduce_precision(gate_matrix, 8, 7)
    gate_rest = gate_matrix - gate_high
    sent = jnp.concatenate(
        [
            ffn_normed,
            gate_high.astype(jnp.bfloat16),
            gate_rest.astype(jnp.bfloat16),
            jnp.zeros((sequence_length, 2 * EXPERTS), jnp.bfloat16),
        ],
        axis=1,
    )
    arrived = rows_of_all(sent)
    token_rows = arrived[:, :model_width]
    spread_gates = dot32(arrived[:, model_width:], expand)
    gate_lin = dot32(token_rows, gate_w)
    up_lin = dot32(token_rows, up_w)
    inner_act = (jax.nn.silu(gate_lin) * up_lin).astype(jnp.bfloat16)
    weighted = (inner_act.astype(jnp.float32) * spread_gates).astype(jnp.bfloat16)
    mixture = summed_rows(dot32(weighted, down_w).astype(jnp.bfloat16))
    retained = (
        stream,
        attn_normed,
        query_matrix,
        key_matrix,
        value_matrix,
        attend_prob,
        attended,
        middle,
        ffn_normed,
        choose,
        gates,
        token_rows,
        spread_gates,
        gate_lin,
        up_lin,
        inner_act,
        weighted,
    )
    return (middle + mixture.astype(jnp.float32), retained)


def backward_layer(
    carried, retained, segment, attention, gains, router, experts, collect
):
    full_query_keyval, full_out = attention
    gain_attn, gain_ffn = gains
    gate_w, up_w, down_w = experts
    (
        stream,
        attn_normed,
        query_matrix,
        key_matrix,
        value_matrix,
        attend_prob,
        attended,
        middle,
        ffn_normed,
        choose,
        gates,
        token_rows,
        spread_gates,
        gate_lin,
        up_lin,
        inner_act,
        weighted,
    ) = retained
    sequence_length, model_width = carried.shape
    carried_rows = rows_of_all(carried.astype(jnp.bfloat16))
    plain_grad = jnp.einsum("td,fd->tf", carried_rows, down_w, preferred_element_type=jnp.float32)
    choice_grads = jnp.dot(
        inner_act.astype(jnp.float32) * plain_grad, collect, precision=highest
    )
    inner_grad = spread_gates * plain_grad
    squashed = jax.nn.sigmoid(gate_lin)
    gate_low = (inner_grad * up_lin * squashed * (1.0 + gate_lin * (1.0 - squashed))).astype(
        jnp.bfloat16
    )
    up_low = (inner_grad * gate_lin * squashed).astype(jnp.bfloat16)
    row_grads = jnp.einsum("tf,df->td", gate_low, gate_w, preferred_element_type=jnp.float32)
    row_grads = row_grads + jnp.einsum(
        "tf,df->td", up_low, up_w, preferred_element_type=jnp.float32
    )
    returned = summed_rows(
        jnp.concatenate(
            [row_grads.astype(jnp.bfloat16), choice_grads.astype(jnp.bfloat16)], axis=1
        )
    ).astype(jnp.float32)
    expert_grads = (
        jnp.einsum("td,tf->df", token_rows, gate_low, preferred_element_type=jnp.float32),
        jnp.einsum("td,tf->df", token_rows, up_low, preferred_element_type=jnp.float32),
        jnp.einsum("tf,td->fd", weighted, carried_rows, preferred_element_type=jnp.float32),
    )
    expert_grads = tuple(grad.astype(jnp.bfloat16) for grad in expert_grads)
    all_choices = jnp.sum(
        returned[:, model_width:].reshape(sequence_length, -1, EXPERTS), axis=1
    )
    gate_grad = jnp.sum(choose * all_choices[:, None, :], axis=-1)
    chosen_grad = gates * (gate_grad - jnp.sum(gates * gate_grad, axis=-1, keepdims=True))
    logit_grad = jnp.sum(choose * chosen_grad[:, :, None], axis=1)
    router_grad = jnp.einsum(
        "sd,se->de", ffn_normed.astype(jnp.float32), logit_grad, precision=highest
    )
    ffn_grad = jnp.einsum("se,de->sd", logit_grad, router.astype(jnp.float32), precision=highest)
    ffn_grad = ffn_grad + returned[:, :model_width]
    middle_grad, gain_ffn_grad = jax.vjp(normed, middle, gain_ffn)[1](ffn_grad)
    middle_grad = middle_grad + carried
    branch_grad = middle_grad.astype(jnp.bfloat16)
    attention_output_grad = jnp.einsum(
        "sd,ed->se", branch_grad, full_out, preferred_element_type=jnp.float32
    ).astype(jnp.bfloat16)
    query_group_size = QUERY_HEADS // KEY_VALUE_HEADS
    grouped_gradient = attention_output_grad.reshape(
        sequence_length, KEY_VALUE_HEADS, query_group_size, HEAD_DIMENSION
    )
    prob_grad = jnp.einsum(
        "qhgd,khd->hgqk", grouped_gradient, value_matrix, preferred_element_type=jnp.float32
    )
    score_grad = (
        attend_prob * (prob_grad - jnp.sum(prob_grad * attend_prob, axis=-1, keepdims=True))
    ).astype(jnp.bfloat16)
    grouped_queries = query_matrix.reshape(
        sequence_length, KEY_VALUE_HEADS, query_group_size, HEAD_DIMENSION
    )
    query_grad = jnp.einsum(
        "hgqk,khd->qhgd", score_grad, key_matrix, preferred_element_type=jnp.float32
    ).reshape(sequence_length, QUERY_HEADS, HEAD_DIMENSION) * HEAD_DIMENSION ** (-0.5)
    key_gradient = jnp.einsum(
        "hgqk,qhgd->khd", score_grad, grouped_queries, preferred_element_type=jnp.float32
    ) * HEAD_DIMENSION ** (-0.5)
    value_gradient = jnp.einsum(
        "hgqk,qhgd->khd",
        attend_prob.astype(jnp.bfloat16),
        grouped_gradient,
        preferred_element_type=jnp.float32,
    )
    back_position = -positions(segment)
    lows = jnp.concatenate(
        [
            rotary_embed(query_grad, back_position).reshape(sequence_length, -1),
            rotary_embed(key_gradient, back_position).reshape(sequence_length, -1),
            value_gradient.reshape(sequence_length, -1),
        ],
        axis=1,
    ).astype(jnp.bfloat16)
    normed_grad = jnp.einsum(
        "se,de->sd", lows, full_query_keyval, preferred_element_type=jnp.float32
    )
    stream_grad, gain_attn_grad = jax.vjp(normed, stream, gain_attn)[1](normed_grad)
    shared = jnp.concatenate(
        [
            jnp.einsum("sd,se->de", attn_normed, lows, preferred_element_type=jnp.float32),
            jnp.einsum("se,sd->ed", attended, branch_grad, preferred_element_type=jnp.float32),
            router_grad,
            gain_attn_grad[:, None],
            gain_ffn_grad[:, None],
            jnp.zeros((model_width, 128 - EXPERTS - 2), jnp.float32),
        ],
        axis=1,
    ).astype(jnp.bfloat16)
    return (stream_grad + middle_grad, shared, expert_grads)


def on_device(
    inputs,
    cotangent,
    segments,
    routes,
    norm_attn,
    w_query,
    key_value_weight,
    w_out,
    norm_ffn,
    w_router,
    w_gate,
    w_up,
    w_down,
):
    layers = lax.axis_size("pipe")
    core = lax.axis_index("pipe")
    part = lax.axis_index("dp")
    parts = lax.axis_size("dp")
    local_experts, model_width, hidden_units = w_gate.shape[1:]
    slice_width = hidden_units // parts
    first_expert = lax.axis_index("expert") * local_experts

    def own(block, axis=0):
        return lax.dynamic_index_in_dim(block, core, axis, keepdims=False)

    stream = own(inputs)[0].astype(jnp.float32)
    carried = own(cotangent)[0].astype(jnp.float32)
    segment = own(segments)[0]
    routing = own(both_layers(routes[0]), 1)[:, 0]
    gains = both_layers(jnp.concatenate([norm_attn, norm_ffn], axis=0))
    router = both_layers(w_router[0])
    query_keyval = layer_pair(
        lax.all_gather(
            jnp.concatenate([w_query[0], key_value_weight[0]], axis=1), "dp", axis=0, tiled=True
        )
    )
    out_full = layer_pair(lax.all_gather(w_out[0], "dp", axis=0, tiled=True))

    def columns(weight):
        piece = lax.dynamic_slice_in_dim(weight[0], part * slice_width, slice_width, 2)
        return piece.transpose(1, 0, 2).reshape(model_width, local_experts * slice_width)

    down_piece = lax.dynamic_slice_in_dim(w_down[0], part * slice_width, slice_width, 1)
    gate_all = layer_pair(columns(w_gate))
    up_all = layer_pair(columns(w_up))
    down_all = layer_pair(down_piece.reshape(local_experts * slice_width, model_width))
    expand = expand_matrix(local_experts, slice_width, first_expert)
    collect = collect_matrix(local_experts, slice_width, first_expert, part, parts)

    def params(layer):
        return (
            (query_keyval[layer], out_full[layer]),
            (gains[layer, 0], gains[layer, 1]),
            router[layer],
            (gate_all[layer], up_all[layer], down_all[layer]),
        )

    results, kept = [], []
    for layer in range(layers):
        stream, retained = forward_layer(stream, segment, routing[layer], *params(layer), expand)
        results.append(stream)
        kept.append(retained)
    grads_in, totals = [None] * layers, [None] * layers
    for layer in reversed(range(layers)):
        carried, shared, expert_grads = backward_layer(
            carried, kept[layer], segment, *params(layer), collect
        )
        grads_in[layer] = carried
        leaves = (shared,) + expert_grads
        totals[layer] = [
            leaf.astype(jnp.float32)
            + lax.ppermute(
                leaf, "pipe", [(other, layer) for other in range(layers) if other != layer]
            ).astype(jnp.float32)
            for leaf in leaves
        ]
    shared, gate_grad, up_grad, down_grad = [
        jnp.where(core == 0, first, second) for first, second in zip(*totals)
    ]
    shared = lax.psum_scatter(
        shared.astype(jnp.bfloat16), "dp", scatter_dimension=0, tiled=True
    )
    shared = lax.psum(shared, "expert").astype(jnp.float32)

    def swap(first, second):
        ours = jnp.where(core == 0, first, second)
        theirs = lax.ppermute(
            jnp.where(core == 0, second, first).astype(jnp.bfloat16), "pipe", [(0, 1), (1, 0)]
        ).astype(jnp.float32)
        return jnp.stack(
            [jnp.where(core == 0, ours, theirs), jnp.where(core == 0, theirs, ours)]
        )

    def expert_layout(grad):
        return grad.reshape(model_width, local_experts, slice_width).transpose(1, 0, 2)[None]

    width = model_width
    return (
        swap(*results)[None, :, None],
        swap(*grads_in)[None, :, None],
        shared[None, :, 3 * width + EXPERTS],
        shared[None, :, :width],
        shared[None, :, width : 2 * width],
        shared[None, :, 2 * width : 3 * width],
        shared[None, :, 3 * width + EXPERTS + 1],
        shared[None, :, 3 * width : 3 * width + EXPERTS],
        expert_layout(gate_grad),
        expert_layout(up_grad),
        down_grad.reshape(1, local_experts, slice_width, model_width),
    )


def solution(mesh):
    return jax.shard_map(
        on_device,
        mesh=mesh,
        in_specs=(
            P(None, ("dp", "expert"), None, None),
            P(None, ("dp", "expert"), None, None),
            P(None, ("dp", "expert"), None),
            P("pipe", None, ("dp", "expert"), None, None),
            P("pipe", None),
            P("pipe", "dp", None),
            P("pipe", "dp", None),
            P("pipe", "dp", None),
            P("pipe", None),
            P("pipe", None, None),
            P("pipe", "expert", None, None),
            P("pipe", "expert", None, None),
            P("pipe", "expert", None, None),
        ),
        out_specs=(
            P("pipe", None, ("dp", "expert"), None, None),
            P("pipe", None, ("dp", "expert"), None, None),
            P("pipe", "dp"),
            P("pipe", "dp", None),
            P("pipe", "dp", None),
            P("pipe", "dp", None),
            P("pipe", "dp"),
            P("pipe", "dp", None),
            P("pipe", "expert", None, "dp"),
            P("pipe", "expert", None, "dp"),
            P("pipe", "expert", "dp", None),
        ),
        check_vma=False,
    )
```
